1024 devices in a mesh: section: 16 (over x, z_hi), dp: 8 (over y, core), head: 8 (over z_lo).
Axes of the slice: x: 4, y: 4, z: 32 (z_hi: 4, z_lo: 8; z = z_hi * 8 + z_lo), core: 2. Of those that a mesh axis runs over, the one named last changes fastest.
Arguments:
- queries: bfloat16 [2, 16, 1024, 12288], P(None, 'section', 'dp', 'head'), may hold values from -40 to 40
- latents: bfloat16 [2, 16, 1024, 576], P(None, 'section', 'dp'), may hold values from -6 to 6
- out_grad: bfloat16 [2, 16, 1024, 8192], P(None, 'section', 'dp', 'head'), may hold values from -6 to 6
- segment_ids: int32 [2, 16, 1024], P(None, 'section', 'dp'), may hold values from 0 to 31, never falling along the last dimension, each value on 1 to 128 neighbouring positions
- up_weight: bfloat16 [2, 16, 512, 16384], P(None, 'section', None, 'head'), may hold values from -0.25 to 0.25
Outputs:
- query_grad: bfloat16 [2, 16, 1024, 12288], P(None, 'section', 'dp', 'head')
- latent_grad: bfloat16 [2, 16, 1024, 576], P(None, 'section', ('dp', 'head'))
- weight_grad: float32 [16, 512, 16384], P('section', 'dp', 'head')
The draws below stay inside these ranges and needn't reach their ends.
All inputs are finite; a program needn't handle non-finite values.
Results may differ from the reference program's by a relative error of at most 0.017.
Values may be sent and summed in bfloat16 or wider, within the bound.
No kernel may reach another device: no remote copies, remote signals or barrier semaphores. Data moves between devices by JAX's collectives and lax.ppermute only.
A program may use at most 64 MiB of HBM per device.

```python
import math
import jax
import jax.numpy as jnp
import numpy as np
from jax import lax

LATENT = 512
ROPE = 64
NOPE = 128
VDIM = 128
HEADS = 64
TOK = 128
SECTIONS = 16
ROWS = 1024
N_DP = 8


def joint_draw(key):
    base = jax.random.fold_in(key, 11)
    first, second = jax.random.split(base, 2)
    query_shape = (2, SECTIONS, ROWS, HEADS, NOPE + ROPE)
    latent_shape = (2, SECTIONS, ROWS, LATENT + ROPE)
    latent_vals = jnp.clip(jax.random.normal(first, latent_shape, jnp.float32), -6.0, 6.0)
    query_vals = jnp.clip(jax.random.normal(second, query_shape, jnp.float32), -6.0, 6.0)
    return (query_vals.reshape(2, SECTIONS, ROWS, HEADS * (NOPE + ROPE)), latent_vals)


def draw_queries(key, part):
    return joint_draw(key)[0].astype(jnp.bfloat16)


def draw_latents(key, part):
    return joint_draw(key)[1].astype(jnp.bfloat16)


def steps_of(own_key, shape, cuts, smallest, high):
    def one(position, shards_of):
        heights = jax.random.uniform(jax.random.fold_in(jax.random.fold_in(own_key, 6), position), (shards_of,), jnp.float32, smallest / len(cuts), high / len(cuts))
        return jnp.repeat(jnp.exp(heights), shape[position] // shards_of).reshape((-1,) + (1,) * (len(shape) - position - 1))

    loudness = one(*cuts[0])
    for cut in cuts[1:]:
        loudness = loudness * one(*cut)
    return loudness


def profile(number_of, total, limit, lean):
    portions = [(1 << 20) // math.isqrt(rank ** lean) + 1 for rank in range(2, number_of + 1)]
    spare, holding = total - limit - (number_of - 1), [1] * (number_of - 1)
    while spare > 0:
        candidates = [i for i in range(number_of - 1) if holding[i] < limit]
        whole, left = sum([portions[i] for i in candidates]), spare
        for i in candidates:
            more = min(limit - holding[i], max(1, left * portions[i] // whole), spare)
            holding[i] = holding[i] + more
            spare = spare - more
    return np.array([limit] + holding)


def uneven(rng, amount, total, bound, skew):
    if amount == 2:
        one = jax.random.randint(rng, (), max(1, total - bound), min(bound, total - 1) + 1)
        return jnp.stack([one, total - one])
    sizes = jnp.asarray(profile(amount, total, bound, skew), jnp.int32)
    twos = (amount - 1) // 2
    donor, receiver = sizes[1:1 + 2 * twos:2], sizes[2:2 + 2 * twos:2]
    slack = jnp.minimum(donor - 1, bound - receiver)
    moved = jax.random.randint(jax.random.fold_in(rng, 1), (twos,), 0, 1 << 20) % (slack + 1)
    sizes = sizes.at[1:1 + 2 * twos:2].set(donor - moved).at[2:2 + 2 * twos:2].set(receiver + moved)
    return sizes[jax.random.permutation(jax.random.fold_in(rng, 2), amount)]


def normal_values(rng, shape, width, reach, cuts=(), held_as=jnp.bfloat16):
    gain = steps_of(rng, shape, cuts, -0.22, 0.18) if cuts else 1.0
    drawn = jax.random.normal(rng, shape, jnp.float32) * width * gain
    return jnp.minimum(jnp.maximum(drawn, -reach), reach).astype(held_as)


def setup_inputs(seed: int = 0) -> dict:
    seeds = jax.random.split(jax.random.key(seed), 6)
    return {
        "queries": draw_queries(jax.random.fold_in(seeds[5], 71), 0),
        "latents": draw_latents(jax.random.fold_in(seeds[5], 71), 0),
        "out_grad": normal_values(seeds[2], (2, SECTIONS, ROWS, HEADS * VDIM), 1.0, 6.0, ((1, 16), (2, 8), (3, 8))),
        "segment_ids": jax.vmap(lambda own: jnp.searchsorted(jnp.cumsum(uneven(own, 4 * N_DP, ROWS, TOK, 1)), jnp.arange(ROWS), side="right"))(jax.random.split(seeds[3], 2 * SECTIONS)).reshape((2, SECTIONS, ROWS)).astype(jnp.int32),
        "up_weight": normal_values(seeds[4], (2, SECTIONS, LATENT, HEADS * (NOPE + VDIM)), LATENT ** -0.5, 0.25, ((1, 16), (3, 8))),
    }


def micro_grads(queries, latents, out_grad, segment_ids, weight):
    tokens = queries.shape[0]
    latent_plain = latents[:, :LATENT]
    key_rope = latents[:, LATENT:].astype(jnp.float32)
    kv_full = jnp.dot(latent_plain, weight, preferred_element_type=jnp.float32).astype(jnp.bfloat16)
    kv_full = kv_full.astype(jnp.float32).reshape(tokens, HEADS, NOPE + VDIM)
    key_plain = kv_full[..., :NOPE]
    values = kv_full[..., NOPE:]
    query_heads = queries.astype(jnp.float32).reshape(tokens, HEADS, NOPE + ROPE)
    query_plain = query_heads[..., :NOPE]
    query_rope = query_heads[..., NOPE:]
    out_heads = out_grad.astype(jnp.float32).reshape(tokens, HEADS, VDIM)
    scale = (NOPE + ROPE) ** -0.5
    scores = (jnp.einsum('thd,shd->hts', query_plain, key_plain) + jnp.einsum('thd,sd->hts', query_rope, key_rope)) * scale
    positions = jnp.arange(tokens)
    allowed = (positions[:, None] >= positions[None, :]) & (segment_ids[:, None] == segment_ids[None, :])
    scores = jnp.where(allowed[None], scores, jnp.float32(-1e30))
    probs = jax.nn.softmax(scores, axis=-1)
    grad_probs = jnp.einsum('thd,shd->hts', out_heads, values)
    delta = jnp.sum(probs * grad_probs, axis=-1, keepdims=True)
    score_grad = (probs * (grad_probs - delta) * scale).astype(jnp.bfloat16).astype(jnp.float32)
    probs_low = probs.astype(jnp.bfloat16).astype(jnp.float32)
    value_grad = jnp.einsum('hts,thd->shd', probs_low, out_heads)
    key_grad = jnp.einsum('hts,thd->shd', score_grad, query_plain)
    rope_grad = jnp.einsum('hts,thd->sd', score_grad, query_rope)
    grad_plain = jnp.einsum('hts,shd->thd', score_grad, key_plain)
    grad_rope = jnp.einsum('hts,sd->thd', score_grad, key_rope)
    query_grad = jnp.concatenate([grad_plain, grad_rope], -1).reshape(tokens, -1).astype(jnp.bfloat16)
    kv_grad = jnp.concatenate([key_grad, value_grad], -1).reshape(tokens, -1).astype(jnp.bfloat16)
    latent_part = jnp.dot(kv_grad, weight.T, preferred_element_type=jnp.float32)
    local_latent = jnp.concatenate([latent_part, rope_grad], 1).astype(jnp.bfloat16)
    partial_value = jnp.dot(latent_plain.T, kv_grad, preferred_element_type=jnp.float32)
    return query_grad, local_latent, partial_value


def direction_grads(queries, latents, out_grad, segment_ids, weights):
    sections = queries.shape[0]
    query_items = queries.reshape(sections, N_DP, TOK, -1)
    latent_items = latents.reshape(sections, N_DP, TOK, -1)
    out_items = out_grad.reshape(sections, N_DP, TOK, -1)
    segment_items = segment_ids.reshape(sections, N_DP, TOK)

    def one_section(items):
        q_section, l_section, o_section, s_section, weight = items

        def step(total, inner):
            query_grad, local_latent, partial_value = micro_grads(inner[0], inner[1], inner[2], inner[3], weight)
            rounded = lax.optimization_barrier(partial_value.astype(jnp.bfloat16)).astype(jnp.float32)
            return total + rounded, (query_grad, local_latent)

        start = jnp.zeros((LATENT, HEADS * (NOPE + VDIM)), jnp.float32)
        total, (query_grads, latent_grads) = lax.scan(step, start, (q_section, l_section, o_section, s_section))
        return query_grads, latent_grads, total

    query_grads, latent_grads, totals = lax.map(one_section, (query_items, latent_items, out_items, segment_items, weights))
    return query_grads.reshape(sections, N_DP * TOK, -1), latent_grads.reshape(sections, N_DP * TOK, -1), totals


def reference(queries, latents, out_grad, segment_ids, up_weight):
    q_fwd, l_fwd, w_fwd = direction_grads(queries[0], latents[0], out_grad[0], segment_ids[0], up_weight[0])
    q_rev, l_rev, w_rev = direction_grads(queries[1], latents[1], out_grad[1], segment_ids[1], up_weight[1])
    q_fwd = jnp.concatenate([q_fwd[1:], jnp.zeros_like(q_fwd[:1])], 0)
    l_fwd = jnp.concatenate([l_fwd[1:], jnp.zeros_like(l_fwd[:1])], 0)
    q_rev = jnp.concatenate([jnp.zeros_like(q_rev[:1]), q_rev[:-1]], 0)
    l_rev = jnp.concatenate([jnp.zeros_like(l_rev[:1]), l_rev[:-1]], 0)
    query_grad = jnp.stack([q_fwd, q_rev], 0)
    latent_grad = jnp.stack([l_fwd, l_rev], 0)
    weight_grad = w_fwd + w_rev[::-1]
    return query_grad, latent_grad, weight_grad
```

```python
import functools

import jax
import jax.numpy as jnp
from jax import lax
from jax.experimental import pallas as pl
from jax.experimental.pallas import tpu as pltpu
from jax.sharding import PartitionSpec as P

LATENT = 512
ROPE = 64
NOPE = 128
VDIM = 128
QDIM = NOPE + ROPE
KVDIM = NOPE + VDIM
F32 = jnp.float32
BF16 = jnp.bfloat16
NT = (((1,), (1,)), ((), ()))
TN = (((0,), (0,)), ((), ()))
NN = (((1,), (0,)), ((), ()))
COST = pl.CostEstimate(flops=1000, bytes_accessed=1000, transcendentals=0)


def dot(a, b, dims):
    return lax.dot_general(a, b, dims, preferred_element_type=F32)


def attention_kernel(side_ref, q_ref, lat_ref, og_ref, seg_ref, w_ref, qg_ref, kvg_ref, rope_ref, allowed_ref):
    step = pl.program_id(0)
    tokens = q_ref.shape[2]

    @pl.when(step == 0)
    def _():
        across = jnp.broadcast_to(seg_ref[0].astype(F32), (tokens, tokens))
        rows = lax.broadcasted_iota(jnp.int32, (tokens, tokens), 0)
        cols = lax.broadcasted_iota(jnp.int32, (tokens, tokens), 1)
        same = (across == across.T) & (rows >= cols)
        allowed_ref[...] = jnp.where(same, 1.0, 0.0)
        rope_ref[...] = jnp.zeros_like(rope_ref)

    allowed = allowed_ref[...] > 0.5
    latents = lat_ref[0, 0]
    plain, key_rope = latents[:, :LATENT], latents[:, LATENT:]
    kv = dot(plain, w_ref[0, 0], NN).astype(BF16)
    scale = QDIM ** (-0.5)
    for h in range(2):
        query = q_ref[0, 0, :, h * QDIM : (h + 1) * QDIM]
        out_grad = og_ref[0, 0, :, h * VDIM : (h + 1) * VDIM]
        key = kv[:, h * KVDIM : h * KVDIM + NOPE]
        value = kv[:, h * KVDIM + NOPE : (h + 1) * KVDIM]
        key_all = jnp.concatenate([key, key_rope], 1)
        scores = jnp.where(allowed, dot(query, key_all, NT) * scale, -1e30)
        powers = jnp.exp(scores - jnp.max(scores, axis=-1, keepdims=True))
        probs = powers / jnp.sum(powers, axis=-1, keepdims=True)
        grad_probs = dot(out_grad, value, NT)
        delta = jnp.sum(probs * grad_probs, axis=-1, keepdims=True)
        score_grad = (probs * (grad_probs - delta) * scale).astype(BF16)
        qg_ref[:, h * QDIM : (h + 1) * QDIM] = dot(score_grad, key_all, NN).astype(BF16)
        key_grad = dot(score_grad, query, TN)
        value_grad = dot(probs.astype(BF16), out_grad, TN)
        kvg_ref[:, h * KVDIM : h * KVDIM + NOPE] = key_grad[:, :NOPE].astype(BF16)
        kvg_ref[:, h * KVDIM + NOPE : (h + 1) * KVDIM] = value_grad.astype(BF16)
        rope_ref[...] += key_grad[:, NOPE:]


def attention(side, queries, latents, out_grad, segment_ids, up_weight):
    tokens, width = queries.shape[2], up_weight.shape[3]
    pairs = width // (2 * KVDIM)
    return pl.pallas_call(
        attention_kernel,
        grid_spec=pltpu.PrefetchScalarGridSpec(
            num_scalar_prefetch=1,
            grid=(pairs,),
            in_specs=[
                pl.BlockSpec((1, 1, tokens, 2 * QDIM), lambda j, s: (s[0], 0, 0, j)),
                pl.BlockSpec((1, 1, tokens, LATENT + ROPE), lambda j, s: (s[0], 0, 0, 0)),
                pl.BlockSpec((1, 1, tokens, 2 * VDIM), lambda j, s: (s[0], 0, 0, j)),
                pl.BlockSpec((1, 1, tokens), lambda j, s: (s[0], 0, 0)),
                pl.BlockSpec((1, 1, LATENT, 2 * KVDIM), lambda j, s: (s[0], 0, 0, j)),
            ],
            out_specs=[
                pl.BlockSpec((tokens, 2 * QDIM), lambda j, s: (0, j)),
                pl.BlockSpec((tokens, 2 * KVDIM), lambda j, s: (0, j)),
                pl.BlockSpec((tokens, ROPE), lambda j, s: (0, 0)),
            ],
            scratch_shapes=[pltpu.VMEM((tokens, tokens), F32)],
        ),
        out_shape=[
            jax.ShapeDtypeStruct((tokens, pairs * 2 * QDIM), BF16),
            jax.ShapeDtypeStruct((tokens, width), BF16),
            jax.ShapeDtypeStruct((tokens, ROPE), F32),
        ],
        compiler_params=pltpu.CompilerParams(vmem_limit_bytes=58 * 1024 * 1024),
        cost_estimate=COST,
    )(side, queries, latents, out_grad, segment_ids, up_weight)


def partial_kernel(who_ref, kvg0_ref, kvg1_ref, rope0_ref, rope1_ref, lat_ref, w0_ref, w1_ref, keep_ref, send_ref, rows_ref, total_ref):
    step = pl.program_id(0)
    first, core = who_ref[0], who_ref[1]
    shard = keep_ref.shape[1] // 4

    @pl.when(step == 0)
    def _():
        total_ref[...] = jnp.zeros_like(total_ref)

    for i, (kvg_ref, w_ref) in enumerate(((kvg0_ref, w0_ref), (kvg1_ref, w1_ref))):
        kv_grad = kvg_ref[...]
        side = first if i == 0 else 1 - first
        plain = lat_ref[side, 0, :, :LATENT]
        part = dot(plain, kv_grad, TN)
        for y in range(4):
            low = part[(2 * y) * shard : (2 * y + 1) * shard]
            high = part[(2 * y + 1) * shard : (2 * y + 2) * shard]
            keep_ref[i, y * shard : (y + 1) * shard, :] = jnp.where(core == 0, low, high).astype(BF16)
            send_ref[i, y * shard : (y + 1) * shard, :] = jnp.where(core == 0, high, low).astype(BF16)
        total_ref[i] += dot(kv_grad, w_ref[0, 0], NT)

    @pl.when(step == pl.num_programs(0) - 1)
    def _():
        for i, rope_ref in enumerate((rope0_ref, rope1_ref)):
            side = first if i == 0 else 1 - first
            rows_ref[side, :, :LATENT] = total_ref[i].astype(BF16)
            rows_ref[side, :, LATENT:] = rope_ref[...].astype(BF16)


def partials(who, kv_grads, ropes, latents, up_weight):
    tokens, width = kv_grads[0].shape
    cols = 512
    return pl.pallas_call(
        partial_kernel,
        grid_spec=pltpu.PrefetchScalarGridSpec(
            num_scalar_prefetch=1,
            grid=(width // cols,),
            in_specs=[
                pl.BlockSpec((tokens, cols), lambda j, s: (0, j)),
                pl.BlockSpec((tokens, cols), lambda j, s: (0, j)),
                pl.BlockSpec((tokens, ROPE), lambda j, s: (0, 0)),
                pl.BlockSpec((tokens, ROPE), lambda j, s: (0, 0)),
                pl.BlockSpec(latents.shape, lambda j, s: (0, 0, 0, 0)),
                pl.BlockSpec((1, 1, LATENT, cols), lambda j, s: (s[0], 0, 0, j)),
                pl.BlockSpec((1, 1, LATENT, cols), lambda j, s: (1 - s[0], 0, 0, j)),
            ],
            out_specs=[
                pl.BlockSpec((2, LATENT // 2, cols), lambda j, s: (0, 0, j)),
                pl.BlockSpec((2, LATENT // 2, cols), lambda j, s: (0, 0, j)),
                pl.BlockSpec((2, tokens, LATENT + ROPE), lambda j, s: (0, 0, 0)),
            ],
            scratch_shapes=[pltpu.VMEM((2, tokens, LATENT), F32)],
        ),
        out_shape=[
            jax.ShapeDtypeStruct((2, LATENT // 2, width), BF16),
            jax.ShapeDtypeStruct((2, LATENT // 2, width), BF16),
            jax.ShapeDtypeStruct((2, tokens, LATENT + ROPE), BF16),
        ],
        compiler_params=pltpu.CompilerParams(vmem_limit_bytes=32 * 1024 * 1024),
        cost_estimate=COST,
    )(who, *kv_grads, *ropes, latents, up_weight, up_weight)


def pair_kernel(y_ref, keep_ref, came_ref, *out_refs):
    shard = out_refs[0].shape[1]
    side = pl.program_id(0)
    for out_ref, (zero, one) in zip(out_refs, ((0, 0), (2, 1), (3, 2), (1, 3))):
        ahead = jnp.where(side == 0, zero, one)
        rows = pl.ds(pl.multiple_of(lax.rem(y_ref[0] + ahead, 4) * shard, shard), shard)
        out_ref[0] = (keep_ref[0, rows, :].astype(F32) + came_ref[0, rows, :].astype(F32)).astype(BF16)


def pair_sums(y, keep, came):
    sides, rows, width = keep.shape
    cols = width // 2
    return pl.pallas_call(
        pair_kernel,
        grid_spec=pltpu.PrefetchScalarGridSpec(
            num_scalar_prefetch=1,
            grid=(sides, width // cols),
            in_specs=[pl.BlockSpec((1, rows, cols), lambda i, j, s: (i, 0, j))] * 2,
            out_specs=[pl.BlockSpec((1, rows // 4, cols), lambda i, j, s: (i, 0, j))] * 4,
        ),
        out_shape=[jax.ShapeDtypeStruct((sides, rows // 4, width), BF16)] * 4,
        compiler_params=pltpu.CompilerParams(vmem_limit_bytes=32 * 1024 * 1024),
        cost_estimate=COST,
    )(y, keep, came)


def placed_kernel(first_ref, one_ref, other_ref, out_ref):
    out_ref[first_ref[0], 0] = one_ref[...]
    out_ref[1 - first_ref[0], 0] = other_ref[...]


def placed(first, arrived):
    rows, width = arrived[0].shape
    cols = width // 4
    return pl.pallas_call(
        placed_kernel,
        grid_spec=pltpu.PrefetchScalarGridSpec(
            num_scalar_prefetch=1,
            grid=(width // cols,),
            in_specs=[pl.BlockSpec((rows, cols), lambda j, s: (0, j))] * 2,
            out_specs=pl.BlockSpec((2, 1, rows, cols), lambda j, s: (0, 0, 0, j)),
        ),
        out_shape=jax.ShapeDtypeStruct((2, 1, rows, width), BF16),
        cost_estimate=COST,
    )(first[None], *arrived)


def total_kernel(after_ref, forward_ref, mirrored_ref, out_ref):
    out_ref[0] = forward_ref[...] + mirrored_ref[...].astype(F32)


def total_of(after, forward, mirrored):
    rows, width = forward.shape
    cols = width // 4
    return pl.pallas_call(
        total_kernel,
        grid=(width // cols,),
        in_specs=[pl.BlockSpec(memory_space=pl.ANY)] + [pl.BlockSpec((rows, cols), lambda j: (0, j))] * 2,
        out_specs=pl.BlockSpec((1, rows, cols), lambda j: (0, 0, j)),
        out_shape=jax.ShapeDtypeStruct((1, rows, width), F32),
        cost_estimate=COST,
    )(after, forward, mirrored)


def relay(block, away):
    sections, heads = lax.axis_size("section"), lax.axis_size("head")
    route = []
    for s in range(sections):
        for h in range(heads):
            there = s - 1 if (h + away) % 2 == 0 else s + 1
            if 0 <= there < sections:
                route.append((s * heads + h, there * heads + h))
    return lax.ppermute(block, ("section", "head"), route)


def sum_over_replicas(first, core, y, kv_grads, ropes, latents, up_weight):
    keep, send, rows = partials(jnp.stack([first, core]), kv_grads, ropes, latents, up_weight)
    came = lax.ppermute(send, "dp", [(i, i ^ 1) for i in range(8)])
    own, up, down, rest = pair_sums(y[None], keep, came)
    above, below = [(i, (i + 2) % 8) for i in range(8)], [(i, (i - 2) % 8) for i in range(8)]
    from_below = lax.ppermute(up, "dp", above).astype(F32)
    from_above = lax.ppermute(down, "dp", below).astype(F32)
    up = (rest[0].astype(F32) + from_below[0]).astype(BF16)
    down = (rest[1].astype(F32) + from_above[1]).astype(BF16)
    up = lax.ppermute(up, "dp", above).astype(F32)
    down = lax.ppermute(down, "dp", below).astype(F32)
    total = (own[0].astype(F32) + from_above[0] + up, own[1].astype(F32) + from_below[1] + down)
    forward = jnp.where(first == 0, total[0], total[1])
    reverse = jnp.where(first == 0, total[1], total[0]).astype(BF16)

    head = lax.axis_index("head")
    part = rows.reshape(2, 8, rows.shape[1] // 8, LATENT + ROPE)
    for bit in range(3):
        part = part.reshape(2, part.shape[1] // 2, 2, *part.shape[2:])
        mine = lax.rem(lax.div(head, 1 << bit), 2)
        sent = jnp.where(mine == 0, part[:, :, 1], part[:, :, 0]).astype(BF16)
        kept = jnp.where(mine == 0, part[:, :, 0], part[:, :, 1]).astype(F32)
        part = kept + lax.ppermute(sent, "head", [(i, i ^ (1 << bit)) for i in range(8)]).astype(F32)
    part = part[:, 0].astype(BF16)
    return forward, reverse, jnp.where(first == 0, part[0], part[1]), jnp.where(first == 0, part[1], part[0])


def body(queries, latents, out_grad, segment_ids, up_weight):
    head, dp = lax.axis_index("head"), lax.axis_index("dp")
    first = lax.rem(head, 2).astype(jnp.int32)
    core, y = lax.rem(dp, 2).astype(jnp.int32), lax.div(dp, 2).astype(jnp.int32)
    sections = lax.axis_size("section")

    results, arrived = [], []
    for i in range(2):
        side = (first if i == 0 else 1 - first)[None]
        results.append(attention(side, queries, latents, out_grad, segment_ids, up_weight))
        arrived.append(relay(results[i][0], i))

    sums = functools.partial(sum_over_replicas, first, core, y)
    operands = ([r[1] for r in results], [r[2] for r in results], latents, up_weight)
    nothing = jax.tree.map(lambda a: jnp.zeros(a.shape, a.dtype), jax.eval_shape(sums, *operands))
    forward, reverse, *parts = lax.cond(segment_ids[0, 0, 0] >= 0, sums, lambda *_: nothing, *operands)

    mirrored = lax.ppermute(reverse, "section", [(i, sections - 1 - i) for i in range(sections)])
    query_grad = placed(first, arrived)
    weight_grad = total_of(query_grad, forward, mirrored)
    latent_arrived = [relay(parts[i], i) for i in range(2)]

    def in_order(pair):
        return jnp.stack([jnp.where(first == 0, pair[0], pair[1]), jnp.where(first == 0, pair[1], pair[0])], 0)[:, None]

    return (query_grad, in_order(latent_arrived), weight_grad)


def solution(mesh):
    in_specs = (
        P(None, "section", "dp", "head"),
        P(None, "section", "dp", None),
        P(None, "section", "dp", "head"),
        P(None, "section", "dp"),
        P(None, "section", None, "head"),
    )
    out_specs = (
        P(None, "section", "dp", "head"),
        P(None, "section", ("dp", "head"), None),
        P("section", "dp", "head"),
    )
    return jax.shard_map(body, mesh=mesh, in_specs=in_specs, out_specs=out_specs, check_vma=False)
```

```python
import functools

import jax
import jax.numpy as jnp
from jax import lax
from jax.experimental import pallas as pl
from jax.experimental.pallas import tpu as pltpu
from jax.sharding import PartitionSpec as P

LATENT = 512
ROPE = 64
NOPE = 128
VDIM = 128
QDIM = NOPE + ROPE
KVDIM = NOPE + VDIM
F32 = jnp.float32
BF16 = jnp.bfloat16
NT = (((1,), (1,)), ((), ()))
TN = (((0,), (0,)), ((), ()))
NN = (((1,), (0,)), ((), ()))
COST = pl.CostEstimate(flops=1000, bytes_accessed=1000, transcendentals=0)


def dot(a, b, dims):
    return lax.dot_general(a, b, dims, preferred_element_type=F32)


def attention_kernel(side_ref, q_ref, lat_ref, og_ref, seg_ref, w_ref, qg_ref, kvg_ref, rows_ref, allowed_ref, rope_ref, total_ref):
    step = pl.program_id(0)
    tokens = q_ref.shape[2]

    @pl.when(step == 0)
    def _():
        across = jnp.broadcast_to(seg_ref[0].astype(F32), (tokens, tokens))
        rows = lax.broadcasted_iota(jnp.int32, (tokens, tokens), 0)
        cols = lax.broadcasted_iota(jnp.int32, (tokens, tokens), 1)
        same = (across == across.T) & (rows >= cols)
        allowed_ref[...] = jnp.where(same, 1.0, 0.0)
        rope_ref[...] = jnp.zeros_like(rope_ref)
        total_ref[...] = jnp.zeros_like(total_ref)

    allowed = allowed_ref[...] > 0.5
    latents = lat_ref[0, 0]
    plain, key_rope = latents[:, :LATENT], latents[:, LATENT:]
    kv = dot(plain, w_ref[0, 0], NN).astype(BF16)
    scale = QDIM ** (-0.5)
    for h in range(2):
        query = q_ref[0, 0, :, h * QDIM : (h + 1) * QDIM]
        out_grad = og_ref[0, 0, :, h * VDIM : (h + 1) * VDIM]
        key = kv[:, h * KVDIM : h * KVDIM + NOPE]
        value = kv[:, h * KVDIM + NOPE : (h + 1) * KVDIM]
        key_all = jnp.concatenate([key, key_rope], 1)
        scores = jnp.where(allowed, dot(query, key_all, NT) * scale, -1e30)
        powers = jnp.exp(scores - jnp.max(scores, axis=-1, keepdims=True))
        probs = powers / jnp.sum(powers, axis=-1, keepdims=True)
        grad_probs = dot(out_grad, value, NT)
        delta = jnp.sum(probs * grad_probs, axis=-1, keepdims=True)
        score_grad = (probs * (grad_probs - delta) * scale).astype(BF16)
        qg_ref[:, h * QDIM : (h + 1) * QDIM] = dot(score_grad, key_all, NN).astype(BF16)
        key_grad = dot(score_grad, query, TN)
        value_grad = dot(probs.astype(BF16), out_grad, TN)
        kvg_ref[:, h * KVDIM : h * KVDIM + NOPE] = key_grad[:, :NOPE].astype(BF16)
        kvg_ref[:, h * KVDIM + NOPE : (h + 1) * KVDIM] = value_grad.astype(BF16)
        rope_ref[...] += key_grad[:, NOPE:]
    total_ref[...] += dot(kvg_ref[...], w_ref[0, 0], NT)

    @pl.when(step == pl.num_programs(0) - 1)
    def _():
        rows_ref[:, :LATENT] = total_ref[...].astype(BF16)
        rows_ref[:, LATENT:] = rope_ref[...].astype(BF16)


def attention(side, queries, latents, out_grad, segment_ids, up_weight):
    tokens, width = queries.shape[2], up_weight.shape[3]
    pairs = width // (2 * KVDIM)
    return pl.pallas_call(
        attention_kernel,
        grid_spec=pltpu.PrefetchScalarGridSpec(
            num_scalar_prefetch=1,
            grid=(pairs,),
            in_specs=[
                pl.BlockSpec((1, 1, tokens, 2 * QDIM), lambda j, s: (s[0], 0, 0, j)),
                pl.BlockSpec((1, 1, tokens, LATENT + ROPE), lambda j, s: (s[0], 0, 0, 0)),
                pl.BlockSpec((1, 1, tokens, 2 * VDIM), lambda j, s: (s[0], 0, 0, j)),
                pl.BlockSpec((1, 1, tokens), lambda j, s: (s[0], 0, 0)),
                pl.BlockSpec((1, 1, LATENT, 2 * KVDIM), lambda j, s: (s[0], 0, 0, j)),
            ],
            out_specs=[
                pl.BlockSpec((tokens, 2 * QDIM), lambda j, s: (0, j)),
                pl.BlockSpec((tokens, 2 * KVDIM), lambda j, s: (0, j)),
                pl.BlockSpec((tokens, LATENT + ROPE), lambda j, s: (0, 0)),
            ],
            scratch_shapes=[
                pltpu.VMEM((tokens, tokens), F32),
                pltpu.VMEM((tokens, ROPE), F32),
                pltpu.VMEM((tokens, LATENT), F32),
            ],
        ),
        out_shape=[
            jax.ShapeDtypeStruct((tokens, pairs * 2 * QDIM), BF16),
            jax.ShapeDtypeStruct((tokens, width), BF16),
            jax.ShapeDtypeStruct((tokens, LATENT + ROPE), BF16),
        ],
        compiler_params=pltpu.CompilerParams(vmem_limit_bytes=58 * 1024 * 1024),
        cost_estimate=COST,
    )(side, queries, latents, out_grad, segment_ids, up_weight)


def partial_kernel(who_ref, kvg0_ref, kvg1_ref, lat_ref, keep_ref, send_ref):
    first, core = who_ref[0], who_ref[1]
    shard = keep_ref.shape[1] // 4
    for i, kvg_ref in enumerate((kvg0_ref, kvg1_ref)):
        side = first if i == 0 else 1 - first
        part = dot(lat_ref[side, 0, :, :LATENT], kvg_ref[...], TN)
        for y in range(4):
            low = part[(2 * y) * shard : (2 * y + 1) * shard]
            high = part[(2 * y + 1) * shard : (2 * y + 2) * shard]
            keep_ref[i, y * shard : (y + 1) * shard, :] = jnp.where(core == 0, low, high).astype(BF16)
            send_ref[i, y * shard : (y + 1) * shard, :] = jnp.where(core == 0, high, low).astype(BF16)


def partials(who, kv_grads, latents):
    tokens, width = kv_grads[0].shape
    cols = 512
    return pl.pallas_call(
        partial_kernel,
        grid_spec=pltpu.PrefetchScalarGridSpec(
            num_scalar_prefetch=1,
            grid=(width // cols,),
            in_specs=[
                pl.BlockSpec((tokens, cols), lambda j, s: (0, j)),
                pl.BlockSpec((tokens, cols), lambda j, s: (0, j)),
                pl.BlockSpec(latents.shape, lambda j, s: (0, 0, 0, 0)),
            ],
            out_specs=[
                pl.BlockSpec((2, LATENT // 2, cols), lambda j, s: (0, 0, j)),
                pl.BlockSpec((2, LATENT // 2, cols), lambda j, s: (0, 0, j)),
            ],
        ),
        out_shape=[
            jax.ShapeDtypeStruct((2, LATENT // 2, width), BF16),
            jax.ShapeDtypeStruct((2, LATENT // 2, width), BF16),
        ],
        compiler_params=pltpu.CompilerParams(vmem_limit_bytes=32 * 1024 * 1024),
        cost_estimate=COST,
    )(who, *kv_grads, latents)


def pair_kernel(y_ref, keep_ref, came_ref, *out_refs):
    shard = out_refs[0].shape[1]
    side = pl.program_id(0)
    for out_ref, (zero, one) in zip(out_refs, ((0, 0), (2, 1), (3, 2), (1, 3))):
        ahead = jnp.where(side == 0, zero, one)
        rows = pl.ds(pl.multiple_of(lax.rem(y_ref[0] + ahead, 4) * shard, shard), shard)
        out_ref[0] = (keep_ref[0, rows, :].astype(F32) + came_ref[0, rows, :].astype(F32)).astype(BF16)


def pair_sums(y, keep, came):
    sides, rows, width = keep.shape
    cols = width // 2
    return pl.pallas_call(
        pair_kernel,
        grid_spec=pltpu.PrefetchScalarGridSpec(
            num_scalar_prefetch=1,
            grid=(sides, width // cols),
            in_specs=[pl.BlockSpec((1, rows, cols), lambda i, j, s: (i, 0, j))] * 2,
            out_specs=[pl.BlockSpec((1, rows // 4, cols), lambda i, j, s: (i, 0, j))] * 4,
        ),
        out_shape=[jax.ShapeDtypeStruct((sides, rows // 4, width), BF16)] * 4,
        compiler_params=pltpu.CompilerParams(vmem_limit_bytes=32 * 1024 * 1024),
        cost_estimate=COST,
    )(y, keep, came)


def held_kernel(after_ref, *refs):
    pass


def held(after, arrays):
    anywhere = pl.BlockSpec(memory_space=pl.ANY)
    return pl.pallas_call(
        held_kernel,
        in_specs=[anywhere] * (1 + len(arrays)),
        out_specs=[anywhere] * len(arrays),
        out_shape=[jax.ShapeDtypeStruct(a.shape, a.dtype) for a in arrays],
        input_output_aliases={i + 1: i for i in range(len(arrays))},
        cost_estimate=COST,
    )(after, *arrays)


def placed_kernel(first_ref, one_ref, other_ref, out_ref):
    out_ref[first_ref[0], 0] = one_ref[...]
    out_ref[1 - first_ref[0], 0] = other_ref[...]


def placed(first, arrived):
    rows, width = arrived[0].shape
    cols = width // 4
    return pl.pallas_call(
        placed_kernel,
        grid_spec=pltpu.PrefetchScalarGridSpec(
            num_scalar_prefetch=1,
            grid=(width // cols,),
            in_specs=[pl.BlockSpec((rows, cols), lambda j, s: (0, j))] * 2,
            out_specs=pl.BlockSpec((2, 1, rows, cols), lambda j, s: (0, 0, 0, j)),
        ),
        out_shape=jax.ShapeDtypeStruct((2, 1, rows, width), BF16),
        compiler_params=pltpu.CompilerParams(vmem_limit_bytes=16 * 1024 * 1024),
        cost_estimate=COST,
    )(first[None], *arrived)


def total_kernel(first_ref, after_ref, forward_ref, mirrored_ref, one_ref, other_ref, out_ref, rows_ref):
    out_ref[0] = forward_ref[...] + mirrored_ref[...].astype(F32)
    rows_ref[first_ref[0], 0] = one_ref[...]
    rows_ref[1 - first_ref[0], 0] = other_ref[...]


def total_of(first, after, forward, mirrored, latent_rows):
    rows, width = forward.shape
    cols = width // 2
    few = latent_rows[0].shape
    return pl.pallas_call(
        total_kernel,
        grid_spec=pltpu.PrefetchScalarGridSpec(
            num_scalar_prefetch=1,
            grid=(width // cols,),
            in_specs=[pl.BlockSpec(memory_space=pl.ANY)]
            + [pl.BlockSpec((rows, cols), lambda j, s: (0, j))] * 2
            + [pl.BlockSpec(few, lambda j, s: (0, 0))] * 2,
            out_specs=[
                pl.BlockSpec((1, rows, cols), lambda j, s: (0, 0, j)),
                pl.BlockSpec((2, 1, *few), lambda j, s: (0, 0, 0, 0)),
            ],
        ),
        out_shape=[
            jax.ShapeDtypeStruct((1, rows, width), F32),
            jax.ShapeDtypeStruct((2, 1, *few), BF16),
        ],
        compiler_params=pltpu.CompilerParams(vmem_limit_bytes=16 * 1024 * 1024),
        cost_estimate=COST,
    )(first[None], after, forward, mirrored, *latent_rows)


def relay(block, away):
    sections, heads = lax.axis_size("section"), lax.axis_size("head")
    route = []
    for s in range(sections):
        for h in range(heads):
            there = s - 1 if (h + away) % 2 == 0 else s + 1
            if 0 <= there < sections:
                route.append((s * heads + h, there * heads + h))
    return lax.ppermute(block, ("section", "head"), route)


def sum_over_replicas(first, y, keep, send):
    came = lax.ppermute(send, "dp", [(i, i ^ 1) for i in range(8)])
    own, up, down, rest = pair_sums(y[None], keep, came)
    above, below = [(i, (i + 2) % 8) for i in range(8)], [(i, (i - 2) % 8) for i in range(8)]
    from_below = lax.ppermute(up, "dp", above).astype(F32)
    from_above = lax.ppermute(down, "dp", below).astype(F32)
    up = (rest[0].astype(F32) + from_below[0]).astype(BF16)
    down = (rest[1].astype(F32) + from_above[1]).astype(BF16)
    up = lax.ppermute(up, "dp", above).astype(F32)
    down = lax.ppermute(down, "dp", below).astype(F32)
    total = (own[0].astype(F32) + from_above[0] + up, own[1].astype(F32) + from_below[1] + down)
    forward = jnp.where(first == 0, total[0], total[1])
    reverse = jnp.where(first == 0, total[1], total[0]).astype(BF16)
    return forward, reverse


def sum_over_heads(part):
    head = lax.axis_index("head")
    part = part.reshape(2, 8, part.shape[1] // 8, LATENT + ROPE)
    for bit in range(3):
        part = part.reshape(2, part.shape[1] // 2, 2, *part.shape[2:])
        mine = lax.rem(lax.div(head, 1 << bit), 2)
        sent = jnp.where(mine == 0, part[:, :, 1], part[:, :, 0]).astype(BF16)
        kept = jnp.where(mine == 0, part[:, :, 0], part[:, :, 1]).astype(F32)
        part = kept + lax.ppermute(sent, "head", [(i, i ^ (1 << bit)) for i in range(8)]).astype(F32)
    return part[:, 0].astype(BF16)


def in_order(first, one, other):
    return jnp.stack([jnp.where(first == 0, one, other), jnp.where(first == 0, other, one)], 0)


def body(queries, latents, out_grad, segment_ids, up_weight):
    head, dp = lax.axis_index("head"), lax.axis_index("dp")
    first = lax.rem(head, 2).astype(jnp.int32)
    core, y = lax.rem(dp, 2).astype(jnp.int32), lax.div(dp, 2).astype(jnp.int32)
    sections = lax.axis_size("section")

    query_grads, kv_grads, rows = zip(
        *[
            attention((first if i == 0 else 1 - first)[None], queries, latents, out_grad, segment_ids, up_weight)
            for i in range(2)
        ]
    )
    part = sum_over_heads(in_order(first, *rows))
    part = in_order(first, part[0], part[1])
    keep, send = partials(jnp.stack([first, core]), kv_grads, latents)
    query_grads = held(part, query_grads)
    arrived = [relay(query_grads[i], i) for i in range(2)]
    latent_here = [relay(part[i], i) for i in range(2)]

    sums = functools.partial(sum_over_replicas, first, y)
    nothing = jax.tree.map(lambda a: jnp.zeros(a.shape, a.dtype), jax.eval_shape(sums, keep, send))
    forward, reverse = lax.cond(segment_ids[0, 0, 0] >= 0, sums, lambda *_: nothing, keep, send)

    mirrored = lax.ppermute(reverse, "section", [(i, sections - 1 - i) for i in range(sections)])
    query_grad = placed(first, arrived)
    weight_grad, latent_grad = total_of(first, query_grad, forward, mirrored, latent_here)
    return (query_grad, latent_grad, weight_grad)


def solution(mesh):
    in_specs = (
        P(None, "section", "dp", "head"),
        P(None, "section", "dp", None),
        P(None, "section", "dp", "head"),
        P(None, "section", "dp"),
        P(None, "section", None, "head"),
    )
    out_specs = (
        P(None, "section", "dp", "head"),
        P(None, "section", ("dp", "head"), None),
        P("section", "dp", "head"),
    )
    return jax.shard_map(body, mesh=mesh, in_specs=in_specs, out_specs=out_specs, check_vma=False)
```

```python
import functools

import jax
import jax.numpy as jnp
from jax import lax
from jax.experimental import pallas as pl
from jax.experimental.pallas import tpu as pltpu
from jax.sharding import PartitionSpec as P

LATENT = 512
ROPE = 64
NOPE = 128
VDIM = 128
QDIM = NOPE + ROPE
KVDIM = NOPE + VDIM
F32 = jnp.float32
BF16 = jnp.bfloat16
NT = (((1,), (1,)), ((), ()))
TN = (((0,), (0,)), ((), ()))
NN = (((1,), (0,)), ((), ()))
COST = pl.CostEstimate(flops=1000, bytes_accessed=1000, transcendentals=0)


def dot(a, b, dims):
    return lax.dot_general(a, b, dims, preferred_element_type=F32)


def attention_kernel(first_ref, q_ref, lat_ref, og_ref, seg_ref, w_ref, qg0_ref, qg1_ref, kvg_ref, rows_ref):
    step = pl.program_id(0)
    tokens = q_ref.shape[2]
    heads = range(w_ref.shape[3] // KVDIM)
    across = jnp.broadcast_to(seg_ref[0].astype(F32), (tokens, tokens))
    down = lax.broadcasted_iota(jnp.int32, (tokens, tokens), 0)
    cols = lax.broadcasted_iota(jnp.int32, (tokens, tokens), 1)
    allowed = (across == across.T) & (down >= cols)
    plain, key_rope = lat_ref[0, 0, :LATENT, :].T, lat_ref[0, 0, LATENT:, :].T
    kv = dot(plain, w_ref[0, 0], NN).astype(BF16)
    scale = QDIM ** (-0.5)
    query = [q_ref[0, 0, :, h * QDIM : (h + 1) * QDIM] for h in heads]
    out_grad = [og_ref[0, 0, :, h * VDIM : (h + 1) * VDIM] for h in heads]
    key = [jnp.concatenate([kv[:, h * KVDIM : h * KVDIM + NOPE], key_rope], 1) for h in heads]
    scores = [dot(query[h], key[h], NT) for h in heads]
    grad_probs = [dot(out_grad[h], kv[:, h * KVDIM + NOPE : (h + 1) * KVDIM], NT) for h in heads]
    scores = [jnp.where(allowed, x * scale, -1e30) for x in scores]
    powers = [jnp.exp(x - jnp.max(x, axis=-1, keepdims=True)) for x in scores]
    probs = [x / jnp.sum(x, axis=-1, keepdims=True) for x in powers]
    delta = [jnp.sum(probs[h] * grad_probs[h], axis=-1, keepdims=True) for h in heads]
    score_grad = [(probs[h] * (grad_probs[h] - delta[h]) * scale).astype(BF16) for h in heads]
    query_grad = [dot(score_grad[h], key[h], NN) for h in heads]
    value_grad = [dot(probs[h].astype(BF16), out_grad[h], TN) for h in heads]
    key_grad = [dot(score_grad[h], query[h], TN) for h in heads]
    for h in heads:
        kvg_ref[0, :, h * KVDIM : h * KVDIM + NOPE] = key_grad[h][:, :NOPE].astype(BF16)
        kvg_ref[0, :, h * KVDIM + NOPE : (h + 1) * KVDIM] = value_grad[h].astype(BF16)
    rows_ref[0, :, :LATENT] = dot(kvg_ref[0], w_ref[0, 0], NT).astype(BF16)
    rows_ref[0, :, LATENT:] = sum(x[:, NOPE:] for x in key_grad).astype(BF16)
    for turn, qg_ref in enumerate((qg0_ref, qg1_ref)):

        @pl.when(step == turn)
        def _():
            for h in heads:
                qg_ref[:, h * QDIM : (h + 1) * QDIM] = query_grad[h].astype(BF16)


def attention(first, queries, latents, out_grad, segment_ids, up_weight):
    tokens, width = queries.shape[2], up_weight.shape[3]

    def whole(shape, order):
        return pl.BlockSpec((1, *shape), lambda i, s: (jnp.where(i == 0, s[0], 1 - s[0]) if order else i,) + (0,) * len(shape))

    return pl.pallas_call(
        attention_kernel,
        grid_spec=pltpu.PrefetchScalarGridSpec(
            num_scalar_prefetch=1,
            grid=(2,),
            in_specs=[whole(a.shape[1:], True) for a in (queries, latents, out_grad, segment_ids, up_weight)],
            out_specs=[
                pl.BlockSpec(queries.shape[2:], lambda i, s: (0, 0)),
                pl.BlockSpec(queries.shape[2:], lambda i, s: (0, 0)),
                whole((tokens, width), False),
                whole((tokens, LATENT + ROPE), True),
            ],
        ),
        out_shape=[
            jax.ShapeDtypeStruct(queries.shape[2:], BF16),
            jax.ShapeDtypeStruct(queries.shape[2:], BF16),
            jax.ShapeDtypeStruct((2, tokens, width), BF16),
            jax.ShapeDtypeStruct((2, tokens, LATENT + ROPE), BF16),
        ],
        compiler_params=pltpu.CompilerParams(vmem_limit_bytes=58 * 1024 * 1024),
        cost_estimate=COST,
    )(first, queries, latents, out_grad, segment_ids, up_weight)


def partial_kernel(who_ref, kvg_ref, lat_ref, keep_ref, send_ref):
    first, core = who_ref[0], who_ref[1]
    shard = keep_ref.shape[1] // 4
    for i in range(2):
        side = first if i == 0 else 1 - first
        part = dot(lat_ref[side, 0, :LATENT, :], kvg_ref[i], NN)
        for y in range(4):
            low = part[(2 * y) * shard : (2 * y + 1) * shard]
            high = part[(2 * y + 1) * shard : (2 * y + 2) * shard]
            keep_ref[i, y * shard : (y + 1) * shard, :] = jnp.where(core == 0, low, high).astype(BF16)
            send_ref[i, y * shard : (y + 1) * shard, :] = jnp.where(core == 0, high, low).astype(BF16)


def partials(who, kv_grads, latents):
    tokens, width = kv_grads.shape[1:]
    cols = 512
    return pl.pallas_call(
        partial_kernel,
        grid_spec=pltpu.PrefetchScalarGridSpec(
            num_scalar_prefetch=1,
            grid=(width // cols,),
            in_specs=[
                pl.BlockSpec((2, tokens, cols), lambda j, s: (0, 0, j)),
                pl.BlockSpec(latents.shape, lambda j, s: (0, 0, 0, 0)),
            ],
            out_specs=[
                pl.BlockSpec((2, LATENT // 2, cols), lambda j, s: (0, 0, j)),
                pl.BlockSpec((2, LATENT // 2, cols), lambda j, s: (0, 0, j)),
            ],
        ),
        out_shape=[
            jax.ShapeDtypeStruct((2, LATENT // 2, width), BF16),
            jax.ShapeDtypeStruct((2, LATENT // 2, width), BF16),
        ],
        compiler_params=pltpu.CompilerParams(vmem_limit_bytes=32 * 1024 * 1024),
        cost_estimate=COST,
    )(who, kv_grads, latents)


def pair_kernel(y_ref, keep_ref, came_ref, *out_refs):
    shard = out_refs[0].shape[1]
    side = pl.program_id(0)
    for out_ref, (zero, one) in zip(out_refs, ((0, 0), (2, 1), (3, 2), (1, 3))):
        ahead = jnp.where(side == 0, zero, one)
        rows = pl.ds(pl.multiple_of(lax.rem(y_ref[0] + ahead, 4) * shard, shard), shard)
        out_ref[0] = (keep_ref[0, rows, :].astype(F32) + came_ref[0, rows, :].astype(F32)).astype(BF16)


def pair_sums(y, keep, came):
    sides, rows, width = keep.shape
    cols = width // 2
    return pl.pallas_call(
        pair_kernel,
        grid_spec=pltpu.PrefetchScalarGridSpec(
            num_scalar_prefetch=1,
            grid=(sides, width // cols),
            in_specs=[pl.BlockSpec((1, rows, cols), lambda i, j, s: (i, 0, j))] * 2,
            out_specs=[pl.BlockSpec((1, rows // 4, cols), lambda i, j, s: (i, 0, j))] * 4,
        ),
        out_shape=[jax.ShapeDtypeStruct((sides, rows // 4, width), BF16)] * 4,
        compiler_params=pltpu.CompilerParams(vmem_limit_bytes=32 * 1024 * 1024),
        cost_estimate=COST,
    )(y, keep, came)


def held_kernel(after_ref, *refs):
    pass


def held(after, arrays):
    anywhere = pl.BlockSpec(memory_space=pl.ANY)
    return pl.pallas_call(
        held_kernel,
        in_specs=[anywhere] * (1 + len(arrays)),
        out_specs=[anywhere] * len(arrays),
        out_shape=[jax.ShapeDtypeStruct(a.shape, a.dtype) for a in arrays],
        input_output_aliases={i + 1: i for i in range(len(arrays))},
        cost_estimate=COST,
    )(after, *arrays)


def placed_kernel(first_ref, one_ref, other_ref, out_ref):
    out_ref[first_ref[0], 0] = one_ref[...]
    out_ref[1 - first_ref[0], 0] = other_ref[...]


def placed(first, arrived):
    rows, width = arrived[0].shape
    cols = width // 4
    return pl.pallas_call(
        placed_kernel,
        grid_spec=pltpu.PrefetchScalarGridSpec(
            num_scalar_prefetch=1,
            grid=(width // cols,),
            in_specs=[pl.BlockSpec((rows, cols), lambda j, s: (0, j))] * 2,
            out_specs=pl.BlockSpec((2, 1, rows, cols), lambda j, s: (0, 0, 0, j)),
        ),
        out_shape=jax.ShapeDtypeStruct((2, 1, rows, width), BF16),
        compiler_params=pltpu.CompilerParams(vmem_limit_bytes=16 * 1024 * 1024),
        cost_estimate=COST,
    )(first[None], *arrived)


def total_kernel(first_ref, after_ref, forward_ref, mirrored_ref, one_ref, other_ref, out_ref, rows_ref):
    out_ref[0] = forward_ref[...] + mirrored_ref[...].astype(F32)
    rows_ref[first_ref[0], 0] = one_ref[...]
    rows_ref[1 - first_ref[0], 0] = other_ref[...]


def total_of(first, after, forward, mirrored, latent_rows):
    rows, width = forward.shape
    cols = width // 2
    few = latent_rows[0].shape
    return pl.pallas_call(
        total_kernel,
        grid_spec=pltpu.PrefetchScalarGridSpec(
            num_scalar_prefetch=1,
            grid=(width // cols,),
            in_specs=[pl.BlockSpec(memory_space=pl.ANY)]
            + [pl.BlockSpec((rows, cols), lambda j, s: (0, j))] * 2
            + [pl.BlockSpec(few, lambda j, s: (0, 0))] * 2,
            out_specs=[
                pl.BlockSpec((1, rows, cols), lambda j, s: (0, 0, j)),
                pl.BlockSpec((2, 1, *few), lambda j, s: (0, 0, 0, 0)),
            ],
        ),
        out_shape=[
            jax.ShapeDtypeStruct((1, rows, width), F32),
            jax.ShapeDtypeStruct((2, 1, *few), BF16),
        ],
        compiler_params=pltpu.CompilerParams(vmem_limit_bytes=16 * 1024 * 1024),
        cost_estimate=COST,
    )(first[None], after, forward, mirrored, *latent_rows)


def relay(block, away):
    sections, heads = lax.axis_size("section"), lax.axis_size("head")
    route = []
    for s in range(sections):
        for h in range(heads):
            there = s - 1 if (h + away) % 2 == 0 else s + 1
            if 0 <= there < sections:
                route.append((s * heads + h, there * heads + h))
    return lax.ppermute(block, ("section", "head"), route)


def sum_over_replicas(first, y, keep, send):
    came = lax.ppermute(send, "dp", [(i, i ^ 1) for i in range(8)])
    own, up, down, rest = pair_sums(y[None], keep, came)
    above, below = [(i, (i + 2) % 8) for i in range(8)], [(i, (i - 2) % 8) for i in range(8)]
    from_below = lax.ppermute(up, "dp", above).astype(F32)
    from_above = lax.ppermute(down, "dp", below).astype(F32)
    up = (rest[0].astype(F32) + from_below[0]).astype(BF16)
    down = (rest[1].astype(F32) + from_above[1]).astype(BF16)
    up = lax.ppermute(up, "dp", above).astype(F32)
    down = lax.ppermute(down, "dp", below).astype(F32)
    total = (own[0].astype(F32) + from_above[0] + up, own[1].astype(F32) + from_below[1] + down)
    forward = jnp.where(first == 0, total[0], total[1])
    reverse = jnp.where(first == 0, total[1], total[0]).astype(BF16)
    return forward, reverse


def sum_over_heads(part):
    head = lax.axis_index("head")
    part = part.reshape(2, 8, part.shape[1] // 8, LATENT + ROPE)
    for bit in range(3):
        part = part.reshape(2, part.shape[1] // 2, 2, *part.shape[2:])
        mine = lax.rem(lax.div(head, 1 << bit), 2)
        sent = jnp.where(mine == 0, part[:, :, 1], part[:, :, 0]).astype(BF16)
        kept = jnp.where(mine == 0, part[:, :, 0], part[:, :, 1]).astype(F32)
        part = kept + lax.ppermute(sent, "head", [(i, i ^ (1 << bit)) for i in range(8)]).astype(F32)
    return part[:, 0].astype(BF16)


def in_order(first, one, other):
    return jnp.stack([jnp.where(first == 0, one, other), jnp.where(first == 0, other, one)], 0)


def body(queries, latents, out_grad, segment_ids, up_weight):
    head, dp = lax.axis_index("head"), lax.axis_index("dp")
    first = lax.rem(head, 2).astype(jnp.int32)
    core, y = lax.rem(dp, 2).astype(jnp.int32), lax.div(dp, 2).astype(jnp.int32)
    sections = lax.axis_size("section")

    across = jnp.swapaxes(latents, 2, 3)
    *query_grads, kv_grads, rows = attention(first[None], queries, across, out_grad, segment_ids, up_weight)
    part = sum_over_heads(rows)
    part = in_order(first, part[0], part[1])
    keep, send = partials(jnp.stack([first, core]), kv_grads, across)
    query_grads = held(part, query_grads)
    arrived = [relay(query_grads[i], i) for i in range(2)]
    latent_here = [relay(part[i], i) for i in range(2)]

    sums = functools.partial(sum_over_replicas, first, y)
    nothing = jax.tree.map(lambda a: jnp.zeros(a.shape, a.dtype), jax.eval_shape(sums, keep, send))
    forward, reverse = lax.cond(segment_ids[0, 0, 0] >= 0, sums, lambda *_: nothing, keep, send)

    mirrored = lax.ppermute(reverse, "section", [(i, sections - 1 - i) for i in range(sections)])
    query_grad = placed(first, arrived)
    weight_grad, latent_grad = total_of(first, query_grad, forward, mirrored, latent_here)
    return (query_grad, latent_grad, weight_grad)


def solution(mesh):
    in_specs = (
        P(None, "section", "dp", "head"),
        P(None, "section", "dp", None),
        P(None, "section", "dp", "head"),
        P(None, "section", "dp"),
        P(None, "section", None, "head"),
    )
    out_specs = (
        P(None, "section", "dp", "head"),
        P(None, "section", ("dp", "head"), None),
        P("section", "dp", "head"),
    )
    return jax.shard_map(body, mesh=mesh, in_specs=in_specs, out_specs=out_specs, check_vma=False)
```
